256 devices in a mesh: grp: 32 (over z, y_hi, core), blk: 8 (over x, y_lo).
Axes of the slice: x: 4, y: 4 (y_hi: 2, y_lo: 2; y = y_hi * 2 + y_lo), z: 8, core: 2. Of those that a mesh axis runs over, the one named last changes fastest.
Arguments:
- samples: bfloat16 [8, 256, 268288], P('blk', 'grp'), may hold values from -7 to 7, as said below
- input_gains: float32 [8, 256, 256], P('blk', 'grp'), may hold values from 0.5 to 2
Outputs:
- vis_near: bfloat16 [4, 256, 2, 2048, 256], P(None, 'grp', None, 'blk')
- vis_far: bfloat16 [128, 2, 2048, 256], P('grp', None, 'blk')
The draws below stay inside these ranges and needn't reach their ends.
Inputs may be any that keep to these rules, and one draw needn't show every extreme that they name: `samples`: whole numbers.
All inputs are finite; a program needn't handle non-finite values.
Results may differ from the reference program's by a relative error of at most 0.0054.
Values may be sent and summed in bfloat16 or wider, within the bound.
No kernel may reach another device: no remote copies, remote signals or barrier semaphores. Data moves between devices by JAX's collectives and lax.ppermute only.
A program may use at most 128 MiB of HBM per device.

```python
import math
import jax
import jax.numpy as jnp
from jax import lax

NI = 2048
TAPS = 4
BAND = 256
SPEC = 128
FRAME = 2048
TLEN = 268288
BLOCKS = 8
BLOCK_IN = 256
HALF = 4
CH = 256
CH_PAIR = 4
CH_HALF = 128
N_GRP = 32


def draw_samples(key, part):
    key = jax.random.fold_in(key, 11)
    spread = 3
    common = 4
    total_length = TLEN + FRAME // 2
    sky_signal = jax.random.randint(jax.random.fold_in(key, 1), (total_length,), -common, common + 1)
    delays = jax.random.randint(jax.random.fold_in(key, 2), (BLOCKS, BLOCK_IN), 0, FRAME // 2)
    noise_key = jax.random.fold_in(key, 3)

    def one_block(block_index):
        noise_part = jax.random.randint(jax.random.fold_in(noise_key, block_index), (BLOCK_IN, TLEN), -spread, spread + 1)
        block_delays = lax.dynamic_index_in_dim(delays, block_index, 0, keepdims=False)

        def delayed(start_at):
            return lax.dynamic_slice_in_dim(sky_signal, start_at, TLEN)
        shifted = jax.vmap(delayed)(block_delays)
        return (noise_part + shifted).astype(jnp.float32).astype(jnp.bfloat16)
    return lax.map(one_block, jnp.arange(BLOCKS, dtype=jnp.int32))


def shard_levels(key, shape, cuts, least, high):
    level = 1.0
    for axis_at, blocks in cuts:
        heights = jax.random.uniform(jax.random.fold_in(jax.random.fold_in(key, 6), axis_at), (blocks,), jnp.float32, least / len(cuts), high / len(cuts))
        level = level * jnp.repeat(jnp.exp(heights), shape[axis_at] // blocks).reshape((-1,) + (1,) * (len(shape) - 1 - axis_at))
    return level


def setup_inputs(seed: int = 0) -> dict:
    seeds = jax.random.split(jax.random.key(seed), 3)
    return {
        "samples": draw_samples(jax.random.fold_in(seeds[2], 71), 0),
        "input_gains": jnp.clip(jnp.exp(math.log(2.0) - 1.3862944 * jax.random.uniform(seeds[1], (BLOCKS, BLOCK_IN, CH), jnp.float32) ** shard_levels(seeds[1], (BLOCKS, BLOCK_IN, CH), ((0, 8), (1, 32)), -0.2, 0.2)), 0.5, 2.0),
    }


def prototype_taps():
    length_all = TAPS * FRAME
    position_frac = (jnp.arange(length_all, dtype=jnp.float32) + 0.5) / length_all
    hann_window = 0.5 - 0.5 * jnp.cos(2.0 * jnp.pi * position_frac)
    return (jnp.sinc(TAPS * (position_frac - 0.5)) * hann_window).reshape(TAPS, FRAME)

def channel_table(channels):
    sample_index = jnp.arange(FRAME, dtype=jnp.int32)[:, None]
    channel_index = BAND + jnp.arange(channels, dtype=jnp.int32)[None, :]
    phase_index = sample_index * channel_index % FRAME
    angles = phase_index.astype(jnp.float32) * (2.0 * jnp.pi / FRAME)
    factor = 0.25 / math.sqrt(FRAME)
    stacked = jnp.stack([jnp.cos(angles) * factor, -jnp.sin(angles) * factor], axis=2)
    return stacked.reshape(FRAME, 2 * channels).astype(jnp.bfloat16)

def filter_frames(voltages, spectra_count):
    row_count = voltages.shape[0]
    framed = voltages.reshape(row_count, spectra_count + TAPS - 1, FRAME)
    weights = prototype_taps()
    summed = jnp.zeros((row_count, spectra_count, FRAME), jnp.float32)
    for tap_index in range(TAPS):
        summed = summed + weights[tap_index] * framed[:, tap_index:tap_index + spectra_count, :].astype(jnp.float32)
    return summed.astype(jnp.bfloat16)

def pair_products(block_spectra):
    own_values = block_spectra.astype(jnp.float32)
    inverse = 1.0 / SPEC
    results = []
    for offset in range(HALF + 1):
        partner = jnp.roll(own_values, -offset, axis=0)
        products = jnp.einsum('pais,pbjs->paibj', own_values, partner, precision=lax.Precision.HIGHEST)
        real_part = products[:, 0, :, 0, :] + products[:, 1, :, 1, :]
        imag_part = products[:, 1, :, 0, :] - products[:, 0, :, 1, :]
        results.append((jnp.stack([real_part, imag_part], axis=1) * inverse).astype(jnp.bfloat16))
    return jnp.stack(results, axis=0)

def reference(samples, input_gains):
    dft_table = channel_table(CH)

    def channelize(pieces):
        block_samples, block_gains = pieces
        frames = filter_frames(block_samples, SPEC)
        raw_spectra = jnp.dot(frames.reshape(BLOCK_IN * SPEC, FRAME), dft_table, preferred_element_type=jnp.float32)
        raw_spectra = raw_spectra.reshape(BLOCK_IN, SPEC, CH, 2)
        return (raw_spectra * block_gains[:, None, :, None]).astype(jnp.bfloat16)
    spectra = lax.map(channelize, (samples, input_gains))
    by_channel = jnp.transpose(spectra, (3, 0, 4, 1, 2))
    every_pair = lax.map(pair_products, by_channel)
    vis_near = jnp.transpose(every_pair[:, :HALF], (1, 0, 3, 2, 4, 5)).reshape(HALF, CH, 2, NI, BLOCK_IN)
    far_all = every_pair[:, HALF].reshape(N_GRP, 2, CH_PAIR, BLOCKS, 2, BLOCK_IN, BLOCK_IN)
    far_pieces = [far_all[:, block_index // HALF, :, block_index] for block_index in range(BLOCKS)]
    vis_far = jnp.stack(far_pieces, axis=3).reshape(CH_HALF, 2, NI, BLOCK_IN)
    return (vis_near, vis_far)
```

```python
import math

import jax
import jax.numpy as jnp
import numpy as np
from jax import lax
from jax.experimental import pallas as pl
from jax.experimental.pallas import tpu as pltpu
from jax.sharding import PartitionSpec as P

TAPS = 4
BAND = 256
SPEC = 128
FRAME = 2048
GROUPS = 32
PER = 8
SHARE = 8
ROWS = GROUPS * 2 * PER
LANES = 2 * SPEC
MIB = 1024 * 1024


def prototype_taps():
    position = (np.arange(TAPS * FRAME, dtype=np.float64) + 0.5) / (TAPS * FRAME)
    window = 0.5 - 0.5 * np.cos(2.0 * np.pi * position)
    return (np.sinc(TAPS * (position - 0.5)) * window).reshape(TAPS, FRAME).astype(np.float32)


def channel_table():
    phase = (np.arange(FRAME)[None, :] * (BAND + np.arange(GROUPS * PER))[:, None]) % FRAME
    angles = phase * (2.0 * np.pi / FRAME)
    factor = 0.25 / math.sqrt(FRAME)
    parts = np.stack([np.cos(angles) * factor, -np.sin(angles) * factor], axis=0)
    table = parts.reshape(2, GROUPS, PER, FRAME).transpose(1, 0, 2, 3).reshape(ROWS, FRAME)
    return table.astype(np.float32).astype(jnp.bfloat16)


SAMPLE_CUTS = (0, 19, 35, 51, 67, 83, 99, 115, 131)
COL = 128


def channelize_kernel(samples, table, taps, gains, out, held, rows, frames, turned, sem_in, sem_table):
    parts = len(SAMPLE_CUTS) - 1

    def sample_copy(i):
        span = pl.ds(SAMPLE_CUTS[i], SAMPLE_CUTS[i + 1] - SAMPLE_CUTS[i])
        return pltpu.make_async_copy(samples.at[span], held.at[span], sem_in.at[i])

    table_copy = pltpu.make_async_copy(table, rows, sem_table)
    for i in range(parts):
        sample_copy(i).start()
    table_copy.start()
    for i in range(parts):
        sample_copy(i).wait()
        first = 16 * i

        def one_column(f, carry, first=first):
            lanes = pl.ds(pl.multiple_of(f * COL, COL), COL)
            weights = [jnp.broadcast_to(taps[t : t + 1, lanes], (SHARE, COL)) for t in range(TAPS)]
            window = [held[first + t, :, lanes].astype(jnp.float32) for t in range(TAPS - 1)]
            for s in range(16):
                window.append(held[first + s + TAPS - 1, :, lanes].astype(jnp.float32))
                total = weights[0] * window[0]
                for t in range(1, TAPS):
                    total = total + weights[t] * window[t]
                frames[f, (first + s) * SHARE : (first + s + 1) * SHARE, :] = total
                window = window[1:]
            return carry

        lax.fori_loop(0, FRAME // COL, one_column, 0)
    table_copy.wait()
    scale = jnp.transpose(gains[...])
    for pair in range(SHARE // 2):
        chosen = [
            jnp.concatenate(
                [
                    frames[f, pl.ds(2 * pair + j, SPEC, stride=SHARE), :].astype(jnp.bfloat16)
                    for f in range(FRAME // COL)
                ],
                axis=1,
            )
            for j in range(2)
        ]
        spectra = lax.dot_general(
            rows[...],
            jnp.concatenate(chosen, axis=0),
            (((1,), (1,)), ((), ())),
            preferred_element_type=jnp.float32,
        )
        for j in range(2):
            n = 2 * pair + j
            factor = scale[:, n : n + 1].reshape(GROUPS, 1, PER, 1)
            mine = spectra[:, j * SPEC : (j + 1) * SPEC].reshape(GROUPS, 2, PER, SPEC) * factor
            turned[pl.ds(n, ROWS, stride=SHARE), :] = mine.reshape(ROWS, SPEC)
    whole = turned[...].reshape(GROUPS, 2, PER, SHARE, SPEC)
    for r in range(2):
        out[:, :, :, r * SPEC : (r + 1) * SPEC] = whole[:, r].astype(jnp.bfloat16)


def channelize(samples, gains):
    by_frame = jnp.transpose(samples.reshape(SHARE, SPEC + TAPS - 1, FRAME), (1, 0, 2))
    return pl.pallas_call(
        channelize_kernel,
        out_shape=jax.ShapeDtypeStruct((GROUPS, PER, SHARE, LANES), jnp.bfloat16),
        in_specs=[
            pl.BlockSpec(memory_space=pl.ANY),
            pl.BlockSpec(memory_space=pl.ANY),
            pl.BlockSpec(memory_space=pltpu.VMEM),
            pl.BlockSpec(memory_space=pltpu.VMEM),
        ],
        out_specs=pl.BlockSpec(memory_space=pltpu.VMEM),
        scratch_shapes=[
            pltpu.VMEM((SPEC + TAPS - 1, SHARE, FRAME), jnp.bfloat16),
            pltpu.VMEM((ROWS, FRAME), jnp.bfloat16),
            pltpu.VMEM((FRAME // COL, SPEC * SHARE, COL), jnp.float32),
            pltpu.VMEM((ROWS * SHARE, SPEC), jnp.float32),
            pltpu.SemaphoreType.DMA((len(SAMPLE_CUTS) - 1,)),
            pltpu.SemaphoreType.DMA,
        ],
        compiler_params=pltpu.CompilerParams(vmem_limit_bytes=58 * MIB),
        name="channelize",
    )(by_frame, channel_table(), prototype_taps(), gains)


def correlate_one(own, other, out):
    mine = own[0]
    crossed = jnp.concatenate([mine[:, SPEC:], -mine[:, :SPEC]], axis=1)
    contract = (((1,), (1,)), ((), ()))
    real = lax.dot_general(mine, other, contract, preferred_element_type=jnp.float32)
    imag = lax.dot_general(crossed, other, contract, preferred_element_type=jnp.float32)
    return real * (1.0 / SPEC), imag * (1.0 / SPEC)


def near_kernel(own, other, *rest):
    out = rest[-1]
    real, imag = correlate_one(own, other[0], out)
    out[0, 0, 0] = real.astype(jnp.bfloat16)
    out[0, 0, 1] = imag.astype(jnp.bfloat16)


def near(own, other, offset, half_count, before):
    channels, width, lanes = own.shape
    block = pl.BlockSpec((1, width, lanes), lambda c: (c, 0, 0))
    operands, specs, aliases = [own, other], [block, block], {}
    if before is not None:
        operands.append(before)
        specs.append(pl.BlockSpec(memory_space=pl.ANY))
        aliases = {2: 0}
    flops = 2 * channels * 2 * width * width * lanes
    return pl.pallas_call(
        near_kernel,
        grid=(channels,),
        out_shape=jax.ShapeDtypeStruct((half_count, channels, 2, width, width), jnp.bfloat16),
        in_specs=specs,
        out_specs=pl.BlockSpec((1, 1, 2, width, width), lambda c: (offset, c, 0, 0, 0)),
        input_output_aliases=aliases,
        cost_estimate=pl.CostEstimate(
            flops=flops, bytes_accessed=2 * own.size * 2 + channels * 4 * width * width, transcendentals=0
        ),
        compiler_params=pltpu.CompilerParams(vmem_limit_bytes=16 * MIB),
        name="near%d" % offset,
    )(*operands)


def far_kernel(start, own, other, out):
    real, imag = correlate_one(own, other[0], out)
    out[0, 0] = real.astype(jnp.bfloat16)
    out[0, 1] = imag.astype(jnp.bfloat16)


def far(own, other, start):
    channels, width, lanes = other.shape
    return pl.pallas_call(
        far_kernel,
        grid_spec=pltpu.PrefetchScalarGridSpec(
            num_scalar_prefetch=1,
            grid=(channels,),
            in_specs=[
                pl.BlockSpec((1, width, lanes), lambda c, start: (start[0] + c, 0, 0)),
                pl.BlockSpec((1, width, lanes), lambda c, start: (c, 0, 0)),
            ],
            out_specs=pl.BlockSpec((1, 2, width, width), lambda c, start: (c, 0, 0, 0)),
        ),
        out_shape=jax.ShapeDtypeStruct((channels, 2, width, width), jnp.bfloat16),
        compiler_params=pltpu.CompilerParams(vmem_limit_bytes=16 * MIB),
        name="far",
    )(start.reshape(1), own, other)


def blk_route(step):
    return [(2 * x + l, step(x, l)) for x in range(4) for l in range(2)]


LEFT = blk_route(lambda x, l: 2 * ((x - 1) % 4) + l)
RIGHT = blk_route(lambda x, l: 2 * ((x + 1) % 4) + l)
SWAP = blk_route(lambda x, l: 2 * x + 1 - l)
BACK = blk_route(lambda x, l: (2 * x + l - 1) % 8)
LEFT_ODD = blk_route(lambda x, l: 2 * ((x - l) % 4) + l)


def on_device(samples, input_gains):
    half_count = lax.axis_size("blk") // 2
    half = PER // 2
    position = lax.axis_index("blk")
    mine_start = position // half_count * half
    pieces = channelize(samples[0], input_gains[0])
    pieces = lax.all_to_all(pieces, "grp", split_axis=0, concat_axis=0, tiled=True)
    own = jnp.transpose(pieces, (1, 0, 2, 3)).reshape(PER, GROUPS * SHARE, LANES)
    outgoing = lax.dynamic_slice_in_dim(own, half - mine_start, half, 0)
    second = lax.ppermute(own, "blk", LEFT)
    across = lax.ppermute(own, "blk", SWAP)
    passing = lax.ppermute(outgoing, "blk", RIGHT)
    third = lax.ppermute(second, "blk", BACK)
    first = lax.ppermute(across, "blk", LEFT_ODD)
    arrived = lax.ppermute(passing, "blk", RIGHT)
    vis_near = near(own, own, 0, half_count, None)
    vis_near = near(own, second, 2, half_count, vis_near)
    vis_near = near(own, first, 1, half_count, vis_near)
    vis_near = near(own, third, 3, half_count, vis_near)
    vis_far = far(own, arrived, mine_start)
    return (vis_near, vis_far)


def solution(mesh):
    return jax.shard_map(
        on_device,
        mesh=mesh,
        in_specs=(P("blk", "grp", None), P("blk", "grp", None)),
        out_specs=(P(None, "grp", None, "blk", None), P("grp", None, "blk", None)),
        check_vma=False,
    )
```

```python
import math

import jax
import jax.numpy as jnp
import numpy as np
from jax import lax
from jax.experimental import pallas as pl
from jax.experimental.pallas import tpu as pltpu
from jax.sharding import PartitionSpec as P

TAPS = 4
BAND = 256
SPEC = 128
FRAME = 2048
GROUPS = 32
PER = 8
SHARE = 8
ROWS = GROUPS * 2 * PER
LANES = 2 * SPEC
MIB = 1024 * 1024


def prototype_taps():
    position = (np.arange(TAPS * FRAME, dtype=np.float64) + 0.5) / (TAPS * FRAME)
    window = 0.5 - 0.5 * np.cos(2.0 * np.pi * position)
    return (np.sinc(TAPS * (position - 0.5)) * window).reshape(TAPS, FRAME).astype(np.float32)


def channel_table():
    phase = (np.arange(FRAME)[None, :] * (BAND + np.arange(GROUPS * PER))[:, None]) % FRAME
    angles = phase * (2.0 * np.pi / FRAME)
    factor = 0.25 / math.sqrt(FRAME)
    parts = np.stack([np.cos(angles) * factor, -np.sin(angles) * factor], axis=0)
    table = parts.reshape(2, GROUPS, PER, FRAME).transpose(1, 0, 2, 3).reshape(ROWS, FRAME)
    return table.astype(np.float32).astype(jnp.bfloat16).reshape(GROUPS, 2 * PER, FRAME)


def constant_tables():
    rest = prototype_taps()
    parts = []
    for _ in range(3):
        part = rest.astype(jnp.bfloat16)
        parts.append(part)
        rest = rest - part.astype(np.float32)
    parts.append(np.zeros_like(parts[0]))
    return np.concatenate([channel_table(), np.concatenate(parts, axis=0)[None]], axis=0)


COL = 128
STEP = 512
STEPS = FRAME // STEP
WIDTH = GROUPS * SHARE
VMEM = pltpu.VMEM


def whole_vmem():
    return pl.BlockSpec(memory_space=VMEM)


def far_start():
    half_count = lax.axis_size("blk") // 2
    return lax.axis_index("blk") // half_count * (PER // 2)


def channelize_kernel(samples, table, gains, out, held, rows, frames, total, turned, parts_of_taps, taps, sem_in, sem_table, sem_taps):
    def columns(step):
        return pl.ds(pl.multiple_of(step * STEP, STEP), STEP)

    def sample_copy(step):
        lanes = columns(step)
        return pltpu.make_async_copy(samples.at[:, :, lanes], held.at[:, :, lanes], sem_in.at[step])

    table_copy = pltpu.make_async_copy(table.at[pl.ds(0, GROUPS)], rows, sem_table)
    taps_copy = pltpu.make_async_copy(table.at[GROUPS], parts_of_taps, sem_taps)
    taps_copy.start()
    sample_copy(0).start()
    sample_copy(1).start()
    table_copy.start()
    for step in range(2, STEPS):
        sample_copy(step).start()
    taps_copy.wait()
    split = parts_of_taps[...].astype(jnp.float32)
    taps[...] = split[:TAPS] + (split[TAPS : 2 * TAPS] + split[2 * TAPS : 3 * TAPS])

    def filter_step(step, slot):
        for b in range(STEP // COL):
            lanes = pl.ds(pl.multiple_of(step * STEP + b * COL, COL), COL)
            weights = [jnp.broadcast_to(taps[t : t + 1, lanes], (SHARE, COL)) for t in range(TAPS)]
            window = [held[t, :, lanes].astype(jnp.float32) for t in range(TAPS - 1)]
            for s in range(SPEC):
                window.append(held[s + TAPS - 1, :, lanes].astype(jnp.float32))
                value = weights[0] * window[0]
                for t in range(1, TAPS):
                    value = value + weights[t] * window[t]
                frames[slot, b, s * SHARE : (s + 1) * SHARE, :] = value
                window = window[1:]

    def transform_step(step, slot, first=False):
        chosen = []
        for n in range(SHARE):
            blocks = [frames[slot, b, pl.ds(n, SPEC, stride=SHARE), :] for b in range(STEP // COL)]
            chosen.append(jnp.concatenate([block.astype(jnp.bfloat16) for block in blocks], axis=1))
        product = lax.dot_general(
            rows[:, :, columns(step)].reshape(ROWS, STEP),
            jnp.concatenate(chosen, axis=0),
            (((1,), (1,)), ((), ())),
            preferred_element_type=jnp.float32,
        )
        total[...] = product if first else total[...] + product

    sample_copy(0).wait()
    filter_step(0, 0)
    table_copy.wait()
    sample_copy(1).wait()
    filter_step(1, 1)
    transform_step(0, 0, True)

    def two_steps(j, carry):
        for k in range(2):
            step = 2 * j + 2 + k
            sample_copy(step).wait()
            filter_step(step, k)
            transform_step(step - 1, 1 - k)
        return carry

    lax.fori_loop(0, STEPS // 2 - 1, two_steps, 0)
    transform_step(STEPS - 1, 1)
    scale = jnp.transpose(gains[...]).reshape(GROUPS, PER, SHARE)
    for n in range(SHARE):
        factor = scale[:, :, n : n + 1].reshape(GROUPS, 1, PER, 1)
        mine = total[:, n * SPEC : (n + 1) * SPEC].reshape(GROUPS, 2, PER, SPEC) * factor
        turned[pl.ds(n, ROWS, stride=SHARE), :] = mine.reshape(ROWS, SPEC)
    whole = turned[...].reshape(GROUPS, 2, PER, SHARE, SPEC)
    for r in range(2):
        out[:, :, :, r * SPEC : (r + 1) * SPEC] = whole[:, r].astype(jnp.bfloat16)


def channelize(samples, gains):
    by_frame = jnp.transpose(samples.reshape(SHARE, SPEC + TAPS - 1, FRAME), (1, 0, 2))
    return pl.pallas_call(
        channelize_kernel,
        out_shape=jax.ShapeDtypeStruct((GROUPS, PER, SHARE, LANES), jnp.bfloat16),
        in_specs=[
            pl.BlockSpec(memory_space=pltpu.HBM),
            pl.BlockSpec(memory_space=pltpu.HBM),
            whole_vmem(),
        ],
        out_specs=whole_vmem(),
        scratch_shapes=[
            VMEM((SPEC + TAPS - 1, SHARE, FRAME), jnp.bfloat16),
            VMEM((GROUPS, 2 * PER, FRAME), jnp.bfloat16),
            VMEM((2, STEP // COL, SPEC * SHARE, COL), jnp.float32),
            VMEM((ROWS, SHARE * SPEC), jnp.float32),
            VMEM((ROWS * SHARE, SPEC), jnp.float32),
            VMEM((4 * TAPS, FRAME), jnp.bfloat16),
            VMEM((TAPS, FRAME), jnp.float32),
            pltpu.SemaphoreType.DMA((STEPS,)),
            pltpu.SemaphoreType.DMA,
            pltpu.SemaphoreType.DMA,
        ],
        compiler_params=pltpu.CompilerParams(vmem_limit_bytes=52 * MIB),
        name="channelize",
    )(by_frame, constant_tables(), gains)


def own_kernel(pieces, low, high, outgoing):
    half = PER // 2
    for g in range(GROUPS):
        rows = slice(g * SHARE, (g + 1) * SHARE)
        low[:, rows, :] = pieces[g, :half]
        high[:, rows, :] = pieces[g, half:]

    @pl.when(far_start() == 0)
    def _():
        outgoing[...] = high[...]

    @pl.when(far_start() != 0)
    def _():
        outgoing[...] = low[...]


def own_halves(pieces):
    half = jax.ShapeDtypeStruct((PER // 2, WIDTH, LANES), jnp.bfloat16)
    return pl.pallas_call(
        own_kernel,
        out_shape=(half,) * 3,
        in_specs=[whole_vmem()],
        out_specs=(whole_vmem(),) * 3,
        compiler_params=pltpu.CompilerParams(vmem_limit_bytes=16 * MIB),
        name="own_halves",
    )(pieces)


def correlate_one(mine, other):
    crossed = jnp.concatenate([mine[:, SPEC:], -mine[:, :SPEC]], axis=1)
    contract = (((1,), (1,)), ((), ()))
    real = lax.dot_general(mine, other, contract, preferred_element_type=jnp.float32)
    imag = lax.dot_general(crossed, other, contract, preferred_element_type=jnp.float32)
    return (real * (1.0 / SPEC)).astype(jnp.bfloat16), (imag * (1.0 / SPEC)).astype(jnp.bfloat16)


def correlate(own, items, before, half_count, arrived=None):
    others = [other for _, _, other in items if other is not None]
    has_far = arrived is not None
    half, width, lanes = own[0].shape

    def kernel(*refs):
        refs = list(refs)
        mine = (refs.pop(0), refs.pop(0))
        sources = [mine[part] if other is None else refs.pop(0) for _, part, other in items]
        arrived = refs.pop(0) if has_far else None
        if before is not None:
            refs.pop(0)
        out = refs.pop(0)
        out_far = refs.pop(0) if has_far else None
        results, sems = refs[:2]
        copies = []
        for j, (offset, part, _) in enumerate(items):
            for c in range(half):
                real, imag = correlate_one(mine[part][c], sources[j][c])
                results[j, c, 0] = real
                results[j, c, 1] = imag
                copy = pltpu.make_async_copy(
                    results.at[j, c], out.at[offset, part * half + c], sems.at[j, c]
                )
                copy.start()
                copies.append(copy)
        if has_far:
            far_results, far_sems = refs[2:]
            low = far_start() == 0
            for c in range(half):
                real, imag = correlate_one(jnp.where(low, mine[0][c], mine[1][c]), arrived[c])
                far_results[c, 0] = real
                far_results[c, 1] = imag
                copy = pltpu.make_async_copy(far_results.at[c], out_far.at[c], far_sems.at[c])
                copy.start()
                copies.append(copy)
        for copy in copies:
            copy.wait()

    near_shape = jax.ShapeDtypeStruct((half_count, PER, 2, width, width), jnp.bfloat16)
    far_shape = jax.ShapeDtypeStruct((half, 2, width, width), jnp.bfloat16)
    operands = [*own, *others] + ([arrived] if has_far else [])
    specs = [whole_vmem()] * len(operands)
    aliases = {}
    if before is not None:
        aliases = {len(operands): 0}
        operands.append(before)
        specs.append(pl.BlockSpec(memory_space=pl.ANY))
    count = len(items)
    scratch = [
        VMEM((count, half, 2, width, width), jnp.bfloat16),
        pltpu.SemaphoreType.DMA((count, half)),
    ]
    if has_far:
        scratch += [VMEM((half, 2, width, width), jnp.bfloat16), pltpu.SemaphoreType.DMA((half,))]
    channels = (count + has_far) * half
    return pl.pallas_call(
        kernel,
        out_shape=(near_shape, far_shape) if has_far else near_shape,
        in_specs=specs,
        out_specs=(pl.BlockSpec(memory_space=pl.ANY),) * 2 if has_far else pl.BlockSpec(memory_space=pl.ANY),
        input_output_aliases=aliases,
        scratch_shapes=scratch,
        cost_estimate=pl.CostEstimate(
            flops=channels * 4 * width * width * lanes,
            bytes_accessed=channels * 4 * width * width,
            transcendentals=0,
        ),
        compiler_params=pltpu.CompilerParams(vmem_limit_bytes=24 * MIB),
        name="correlate_" + "_".join(str(offset) for offset, _, _ in items),
    )(*operands)


def blk_route(step):
    return [(2 * x + l, step(x, l)) for x in range(4) for l in range(2)]


LEFT = blk_route(lambda x, l: 2 * ((x - 1) % 4) + l)
RIGHT = blk_route(lambda x, l: 2 * ((x + 1) % 4) + l)
SWAP = blk_route(lambda x, l: 2 * x + 1 - l)
BACK = blk_route(lambda x, l: (2 * x + l - 1) % 8)
LEFT_ODD = blk_route(lambda x, l: 2 * ((x - l) % 4) + l)


def send(block, axis, route):
    return lax.ppermute(block, axis, route)


def all_arrived(*arrays):
    return lax.optimization_barrier(arrays)


def on_device(samples, input_gains):
    half_count = lax.axis_size("blk") // 2
    pieces = channelize(samples[0], input_gains[0])
    pieces = lax.all_to_all(pieces, "grp", split_axis=0, concat_axis=0, tiled=True)
    *own, outgoing = own_halves(pieces)
    across, second, first, third = [], [], [], []
    for part in range(2):
        second.append(send(own[part], "blk", LEFT))
        across.append(send(own[part], "blk", SWAP))
    passing = send(outgoing, "blk", RIGHT)
    for part in range(2):
        across[part], second[part] = all_arrived(across[part], second[part])
        first.append(send(across[part], "blk", LEFT_ODD))
        third.append(send(second[part], "blk", BACK))
    arrived = send(passing, "blk", RIGHT)
    vis_near = correlate(own, [(0, 0, None), (0, 1, None)], None, half_count)
    vis_near = correlate(own, [(2, 0, second[0]), (2, 1, second[1])], vis_near, half_count)
    vis_near = correlate(own, [(1, 0, first[0]), (3, 0, third[0])], vis_near, half_count)
    last = [(1, 1, first[1]), (3, 1, third[1])]
    vis_near, vis_far = correlate(own, last, vis_near, half_count, arrived)
    return (vis_near, vis_far)


def solution(mesh):
    return jax.shard_map(
        on_device,
        mesh=mesh,
        in_specs=(P("blk", "grp", None), P("blk", "grp", None)),
        out_specs=(P(None, "grp", None, "blk", None), P("grp", None, "blk", None)),
        check_vma=False,
    )
```

```python
import math

import jax
import jax.numpy as jnp
import numpy as np
from jax import lax
from jax.experimental import pallas as pl
from jax.experimental.pallas import tpu as pltpu
from jax.sharding import PartitionSpec as P

TAPS = 4
BAND = 256
SPEC = 128
FRAME = 2048
GROUPS = 32
PER = 8
SHARE = 8
ROWS = GROUPS * 2 * PER
LANES = 2 * SPEC
MIB = 1024 * 1024


def prototype_taps():
    position = (np.arange(TAPS * FRAME, dtype=np.float64) + 0.5) / (TAPS * FRAME)
    window = 0.5 - 0.5 * np.cos(2.0 * np.pi * position)
    return (np.sinc(TAPS * (position - 0.5)) * window).reshape(TAPS, FRAME).astype(np.float32)


def channel_table():
    phase = (np.arange(FRAME)[None, :] * (BAND + np.arange(GROUPS * PER))[:, None]) % FRAME
    angles = phase * (2.0 * np.pi / FRAME)
    factor = 0.25 / math.sqrt(FRAME)
    parts = np.stack([np.cos(angles) * factor, -np.sin(angles) * factor], axis=0)
    table = parts.reshape(2, GROUPS, PER, FRAME).transpose(1, 0, 2, 3).reshape(ROWS, FRAME)
    return table.astype(np.float32).astype(jnp.bfloat16).reshape(GROUPS, 2 * PER, FRAME)


def constant_tables():
    rest = prototype_taps()
    parts = []
    for _ in range(3):
        part = rest.astype(jnp.bfloat16)
        parts.append(part)
        rest = rest - part.astype(np.float32)
    parts.append(np.zeros_like(parts[0]))
    return np.concatenate([channel_table(), np.concatenate(parts, axis=0)[None]], axis=0)


COL = 128
STEP = 512
STEPS = FRAME // STEP
WIDTH = GROUPS * SHARE
VMEM = pltpu.VMEM


def whole_vmem():
    return pl.BlockSpec(memory_space=VMEM)


CHUNKS = PER // 2


def blk_place():
    index = lax.axis_index("blk")
    return index // 2, index % 2


def far_half(x):
    return x // 2


def channelize_kernel(samples, table, gains, out, held, rows, frames, total, turned, parts_of_taps, taps, sem_in, sem_table, sem_taps):
    def columns(step):
        return pl.ds(pl.multiple_of(step * STEP, STEP), STEP)

    def sample_copy(step):
        lanes = columns(step)
        return pltpu.make_async_copy(samples.at[:, :, lanes], held.at[:, :, lanes], sem_in.at[step])

    table_copy = pltpu.make_async_copy(table.at[pl.ds(0, GROUPS)], rows, sem_table)
    taps_copy = pltpu.make_async_copy(table.at[GROUPS], parts_of_taps, sem_taps)
    taps_copy.start()
    sample_copy(0).start()
    sample_copy(1).start()
    table_copy.start()
    for step in range(2, STEPS):
        sample_copy(step).start()
    taps_copy.wait()
    split = parts_of_taps[...].astype(jnp.float32)
    taps[...] = split[:TAPS] + (split[TAPS : 2 * TAPS] + split[2 * TAPS : 3 * TAPS])

    def filter_step(step, slot):
        for b in range(STEP // COL):
            lanes = pl.ds(pl.multiple_of(step * STEP + b * COL, COL), COL)
            weights = [jnp.broadcast_to(taps[t : t + 1, lanes], (SHARE, COL)) for t in range(TAPS)]
            window = [held[t, :, lanes].astype(jnp.float32) for t in range(TAPS - 1)]
            for s in range(SPEC):
                window.append(held[s + TAPS - 1, :, lanes].astype(jnp.float32))
                value = weights[0] * window[0]
                for t in range(1, TAPS):
                    value = value + weights[t] * window[t]
                frames[slot, b, s * SHARE : (s + 1) * SHARE, :] = value
                window = window[1:]

    def transform_step(step, slot, first=False):
        chosen = []
        for n in range(SHARE):
            blocks = [frames[slot, b, pl.ds(n, SPEC, stride=SHARE), :] for b in range(STEP // COL)]
            chosen.append(jnp.concatenate([block.astype(jnp.bfloat16) for block in blocks], axis=1))
        product = lax.dot_general(
            rows[:, :, columns(step)].reshape(ROWS, STEP),
            jnp.concatenate(chosen, axis=0),
            (((1,), (1,)), ((), ())),
            preferred_element_type=jnp.float32,
        )
        total[...] = product if first else total[...] + product

    sample_copy(0).wait()
    filter_step(0, 0)
    table_copy.wait()
    sample_copy(1).wait()
    filter_step(1, 1)
    transform_step(0, 0, True)

    def two_steps(j, carry):
        for k in range(2):
            step = 2 * j + 2 + k
            sample_copy(step).wait()
            filter_step(step, k)
            transform_step(step - 1, 1 - k)
        return carry

    lax.fori_loop(0, STEPS // 2 - 1, two_steps, 0)
    transform_step(STEPS - 1, 1)
    scale = jnp.transpose(gains[...]).reshape(GROUPS, PER, SHARE)
    for n in range(SHARE):
        factor = scale[:, :, n : n + 1].reshape(GROUPS, 1, PER, 1)
        mine = total[:, n * SPEC : (n + 1) * SPEC].reshape(GROUPS, 2, PER, SPEC) * factor
        turned[pl.ds(n, ROWS, stride=SHARE), :] = mine.reshape(ROWS, SPEC)
    whole = turned[...].reshape(GROUPS, 2, PER, SHARE, SPEC)
    for r in range(2):
        out[:, :, :, r * SPEC : (r + 1) * SPEC] = whole[:, r].astype(jnp.bfloat16)


def channelize(samples, gains):
    by_frame = jnp.transpose(samples.reshape(SHARE, SPEC + TAPS - 1, FRAME), (1, 0, 2))
    return pl.pallas_call(
        channelize_kernel,
        out_shape=jax.ShapeDtypeStruct((GROUPS, PER, SHARE, LANES), jnp.bfloat16),
        in_specs=[
            pl.BlockSpec(memory_space=pltpu.HBM),
            pl.BlockSpec(memory_space=pltpu.HBM),
            whole_vmem(),
        ],
        out_specs=whole_vmem(),
        scratch_shapes=[
            VMEM((SPEC + TAPS - 1, SHARE, FRAME), jnp.bfloat16),
            VMEM((GROUPS, 2 * PER, FRAME), jnp.bfloat16),
            VMEM((2, STEP // COL, SPEC * SHARE, COL), jnp.float32),
            VMEM((ROWS, SHARE * SPEC), jnp.float32),
            VMEM((ROWS * SHARE, SPEC), jnp.float32),
            VMEM((4 * TAPS, FRAME), jnp.bfloat16),
            VMEM((TAPS, FRAME), jnp.float32),
            pltpu.SemaphoreType.DMA((STEPS,)),
            pltpu.SemaphoreType.DMA,
            pltpu.SemaphoreType.DMA,
        ],
        compiler_params=pltpu.CompilerParams(vmem_limit_bytes=52 * MIB),
        name="channelize",
    )(by_frame, constant_tables(), gains)


def small_kernel(kernel, name, out_shape, *operands):
    return pl.pallas_call(
        kernel,
        out_shape=out_shape,
        in_specs=[whole_vmem()] * len(operands),
        out_specs=jax.tree.map(lambda _: whole_vmem(), out_shape),
        compiler_params=pltpu.CompilerParams(vmem_limit_bytes=16 * MIB),
        name=name,
    )(*operands)


def blocks(*lead):
    return jax.ShapeDtypeStruct((*lead, WIDTH, LANES), jnp.bfloat16)


def own_kernel(pieces, *outs):
    chunks, outgoing = outs[:CHUNKS], outs[CHUNKS]
    for g in range(GROUPS):
        rows = slice(g * SHARE, (g + 1) * SHARE)
        for i in range(CHUNKS):
            for k in range(2):
                chunks[i][k, rows, :] = pieces[g, CHUNKS * k + i]
    theirs = 1 - far_half(blk_place()[0])
    for i in range(CHUNKS):
        outgoing[i] = chunks[i][theirs]


def own_chunks(pieces):
    shapes = (blocks(2),) * CHUNKS + (blocks(CHUNKS),)
    return small_kernel(own_kernel, "own_chunks", shapes, pieces)


def pass_next(nexts, chosen):
    def kernel(*refs):
        theirs = 1 - far_half((blk_place()[0] + 3) % 4)
        for j in range(len(chosen)):
            refs[-1][j] = refs[j][theirs]

    return small_kernel(kernel, "pass_next", blocks(len(chosen)), *[nexts[i] for i in chosen])


def across_kernel(second, own, out):
    out[...] = jnp.where(blk_place()[1] == 0, second[...], own[...])


def for_across(second, own):
    return small_kernel(across_kernel, "for_across", blocks(2), second, own)


def pass_half_kernel(arrived, *refs):
    seconds, out = refs[:-1], refs[-1]
    x, l = blk_place()
    for i in range(CHUNKS):
        out[i] = jnp.where(l == 0, arrived[i], seconds[i][far_half(x)])


def pass_half(arrived, seconds):
    return small_kernel(pass_half_kernel, "pass_half", blocks(CHUNKS), arrived, *seconds)


def correlate_one(mine, other):
    crossed = jnp.concatenate([mine[:, SPEC:], -mine[:, :SPEC]], axis=1)
    contract = (((1,), (1,)), ((), ()))
    real = lax.dot_general(mine, other, contract, preferred_element_type=jnp.float32)
    imag = lax.dot_general(crossed, other, contract, preferred_element_type=jnp.float32)
    return (real * (1.0 / SPEC)).astype(jnp.bfloat16), (imag * (1.0 / SPEC)).astype(jnp.bfloat16)


def correlate(name, own, arrays, jobs, before, half_count, with_far=False):
    width, lanes = own[0].shape[1:]
    count = len(list(jobs(arrays, True)))

    def kernel(*refs):
        refs = list(refs)
        mine = [refs.pop(0) for _ in own]
        sources = [refs.pop(0) for _ in arrays]
        if before is not None:
            refs.pop(0)
        out = refs.pop(0)
        out_far = refs.pop(0) if with_far else None
        results, sems = refs
        copies = []
        for j, (i, k, other, offset) in enumerate(jobs(sources, False)):
            real, imag = correlate_one(mine[i][k], other)
            results[j, 0] = real
            results[j, 1] = imag
            target = out_far.at[i] if offset is None else out.at[offset, CHUNKS * k + i]
            copy = pltpu.make_async_copy(results.at[j], target, sems.at[j])
            copy.start()
            copies.append(copy)
        for copy in copies:
            copy.wait()

    near_shape = jax.ShapeDtypeStruct((half_count, PER, 2, width, width), jnp.bfloat16)
    far_shape = jax.ShapeDtypeStruct((CHUNKS, 2, width, width), jnp.bfloat16)
    operands = [*own, *arrays]
    specs = [whole_vmem()] * len(operands)
    aliases = {}
    if before is not None:
        aliases = {len(operands): 0}
        operands.append(before)
        specs.append(pl.BlockSpec(memory_space=pl.ANY))
    return pl.pallas_call(
        kernel,
        out_shape=(near_shape, far_shape) if with_far else near_shape,
        in_specs=specs,
        out_specs=(pl.BlockSpec(memory_space=pl.ANY),) * 2 if with_far else pl.BlockSpec(memory_space=pl.ANY),
        input_output_aliases=aliases,
        scratch_shapes=[VMEM((count, 2, width, width), jnp.bfloat16), pltpu.SemaphoreType.DMA((count,))],
        cost_estimate=pl.CostEstimate(
            flops=count * 4 * width * width * lanes,
            bytes_accessed=count * 4 * width * width,
            transcendentals=0,
        ),
        compiler_params=pltpu.CompilerParams(vmem_limit_bytes=24 * MIB),
        name=name,
    )(*operands)


def blk_route(step):
    return [(2 * x + l, step(x, l)) for x in range(4) for l in range(2)]


LEFT = blk_route(lambda x, l: 2 * ((x - 1) % 4) + l)
RIGHT = blk_route(lambda x, l: 2 * ((x + 1) % 4) + l)
SWAP = blk_route(lambda x, l: 2 * x + 1 - l)
LEFT_ODD = blk_route(lambda x, l: 2 * ((x - l) % 4) + l)


def send(block, axis, route):
    return lax.ppermute(block, axis, route)


def all_arrived(*arrays):
    return lax.optimization_barrier(arrays)


def on_device(samples, input_gains):
    half_count = lax.axis_size("blk") // 2
    last = CHUNKS - 1
    pieces = channelize(samples[0], input_gains[0])
    pieces = lax.all_to_all(pieces, "grp", split_axis=0, concat_axis=0, tiled=True)
    *own, outgoing = own_chunks(pieces)
    leaving = list(own)
    across = send(own[last], "blk", SWAP)
    passing = send(outgoing, "blk", RIGHT)
    second, nexts = [], []
    for i in range(CHUNKS):
        second.append(send(leaving[i], "blk", LEFT))
        if i == 0:
            second[i], leaving[2], leaving[3] = all_arrived(second[i], leaving[2], leaving[3])
        if i == 1:
            second[i], passing = all_arrived(second[i], passing)
        if i == 2:
            second[i], *nexts = all_arrived(second[i], *nexts)
        if i < last:
            nexts.append(send(for_across(second[i], own[i]), "blk", SWAP))
    nexts.append(send(across, "blk", LEFT_ODD))
    arrived = send(passing, "blk", RIGHT)
    third_a = send(pass_next(nexts, (0, 1)), "blk", LEFT)
    third_b = send(pass_next(nexts, (2, 3)), "blk", LEFT)
    third_half = send(pass_half(arrived, second), "blk", SWAP)

    def same(refs, counting):
        for i in range(CHUNKS):
            for k in range(2):
                yield i, k, None if counting else refs[i][k], 0

    def second_and_far(refs, counting):
        for i in range(CHUNKS):
            for k in range(2):
                yield i, k, None if counting else refs[i][k], 2
        half = None if counting else far_half(blk_place()[0])
        for i in range(CHUNKS):
            yield i, half, None if counting else refs[CHUNKS][i], None

    def first(refs, counting):
        for i in range(CHUNKS):
            for k in range(2):
                yield i, k, None if counting else refs[i][k], 1

    def third(refs, counting):
        half = None if counting else far_half(blk_place()[0])
        for i in range(CHUNKS):
            yield i, None if counting else 1 - half, None if counting else refs[i // 2][i % 2], 3
        for i in range(CHUNKS):
            yield i, half, None if counting else refs[2][i], 3

    vis_near = correlate("correlate_same", own, own, same, None, half_count)
    vis_near, vis_far = correlate(
        "correlate_second", own, [*second, arrived], second_and_far, vis_near, half_count, True
    )
    vis_near = correlate("correlate_first", own, nexts, first, vis_near, half_count)
    vis_near = correlate("correlate_third", own, [third_a, third_b, third_half], third, vis_near, half_count)
    return (vis_near, vis_far)


def solution(mesh):
    return jax.shard_map(
        on_device,
        mesh=mesh,
        in_specs=(P("blk", "grp", None), P("blk", "grp", None)),
        out_specs=(P(None, "grp", None, "blk", None), P("grp", None, "blk", None)),
        check_vma=False,
    )
```

```python
import math

import jax
import jax.numpy as jnp
import numpy as np
from jax import lax
from jax.experimental import pallas as pl
from jax.experimental.pallas import tpu as pltpu
from jax.sharding import PartitionSpec as P

TAPS = 4
BAND = 256
SPEC = 128
FRAME = 2048
GROUPS = 32
PER = 8
SHARE = 8
ROWS = GROUPS * 2 * PER
LANES = 2 * SPEC
MIB = 1024 * 1024


def prototype_taps():
    position = (np.arange(TAPS * FRAME, dtype=np.float64) + 0.5) / (TAPS * FRAME)
    window = 0.5 - 0.5 * np.cos(2.0 * np.pi * position)
    return (np.sinc(TAPS * (position - 0.5)) * window).reshape(TAPS, FRAME).astype(np.float32)


def channel_table():
    phase = (np.arange(FRAME)[None, :] * (BAND + np.arange(GROUPS * PER))[:, None]) % FRAME
    angles = phase * (2.0 * np.pi / FRAME)
    factor = 0.25 / math.sqrt(FRAME)
    parts = np.stack([np.cos(angles) * factor, -np.sin(angles) * factor], axis=0)
    table = parts.reshape(2, GROUPS, PER, FRAME).transpose(1, 0, 2, 3).reshape(ROWS, FRAME)
    return table.astype(np.float32).astype(jnp.bfloat16).reshape(GROUPS, 2 * PER, FRAME)


def constant_tables():
    rest = prototype_taps()
    parts = []
    for _ in range(3):
        part = rest.astype(jnp.bfloat16)
        parts.append(part)
        rest = rest - part.astype(np.float32)
    parts.append(np.zeros_like(parts[0]))
    return np.concatenate([channel_table(), np.concatenate(parts, axis=0)[None]], axis=0)


COL = 128
STEP = 512
STEPS = FRAME // STEP
WIDTH = GROUPS * SHARE
VMEM = pltpu.VMEM


def whole_vmem():
    return pl.BlockSpec(memory_space=VMEM)


CHUNKS = PER // 2


def blk_place():
    index = lax.axis_index("blk")
    return index // 2, index % 2


def far_half(x):
    return x // 2


def channelize_kernel(samples, table, gains, out, held, rows, frames, total, turned, parts_of_taps, taps, sem_in, sem_table, sem_taps):
    def columns(step):
        return pl.ds(pl.multiple_of(step * STEP, STEP), STEP)

    def sample_copy(step):
        lanes = columns(step)
        return pltpu.make_async_copy(samples.at[:, :, lanes], held.at[:, :, lanes], sem_in.at[step])

    table_copy = pltpu.make_async_copy(table.at[pl.ds(0, GROUPS)], rows, sem_table)
    taps_copy = pltpu.make_async_copy(table.at[GROUPS], parts_of_taps, sem_taps)
    taps_copy.start()
    sample_copy(0).start()
    sample_copy(1).start()
    table_copy.start()
    for step in range(2, STEPS):
        sample_copy(step).start()
    taps_copy.wait()
    split = parts_of_taps[...].astype(jnp.float32)
    taps[...] = split[:TAPS] + (split[TAPS : 2 * TAPS] + split[2 * TAPS : 3 * TAPS])

    def filter_step(step, slot):
        for b in range(STEP // COL):
            lanes = pl.ds(pl.multiple_of(step * STEP + b * COL, COL), COL)
            weights = [jnp.broadcast_to(taps[t : t + 1, lanes], (SHARE, COL)) for t in range(TAPS)]
            window = [held[t, :, lanes].astype(jnp.float32) for t in range(TAPS - 1)]
            for s in range(SPEC):
                window.append(held[s + TAPS - 1, :, lanes].astype(jnp.float32))
                value = weights[0] * window[0]
                for t in range(1, TAPS):
                    value = value + weights[t] * window[t]
                frames[slot, b, s * SHARE : (s + 1) * SHARE, :] = value
                window = window[1:]

    def transform_step(step, slot, first=False):
        chosen = []
        for n in range(SHARE):
            blocks = [frames[slot, b, pl.ds(n, SPEC, stride=SHARE), :] for b in range(STEP // COL)]
            chosen.append(jnp.concatenate([block.astype(jnp.bfloat16) for block in blocks], axis=1))
        product = lax.dot_general(
            rows[:, :, columns(step)].reshape(ROWS, STEP),
            jnp.concatenate(chosen, axis=0),
            (((1,), (1,)), ((), ())),
            preferred_element_type=jnp.float32,
        )
        total[...] = product if first else total[...] + product

    sample_copy(0).wait()
    filter_step(0, 0)
    table_copy.wait()
    sample_copy(1).wait()
    filter_step(1, 1)
    transform_step(0, 0, True)

    def two_steps(j, carry):
        for k in range(2):
            step = 2 * j + 2 + k
            sample_copy(step).wait()
            filter_step(step, k)
            transform_step(step - 1, 1 - k)
        return carry

    lax.fori_loop(0, STEPS // 2 - 1, two_steps, 0)
    transform_step(STEPS - 1, 1)
    scale = jnp.transpose(gains[...]).reshape(GROUPS, PER, SHARE)
    for n in range(SHARE):
        factor = scale[:, :, n : n + 1].reshape(GROUPS, 1, PER, 1)
        mine = total[:, n * SPEC : (n + 1) * SPEC].reshape(GROUPS, 2, PER, SPEC) * factor
        turned[pl.ds(n, ROWS, stride=SHARE), :] = mine.reshape(ROWS, SPEC)
    whole = turned[...].reshape(GROUPS, 2, PER, SHARE, SPEC)
    for r in range(2):
        out[:, :, :, r * SPEC : (r + 1) * SPEC] = whole[:, r].astype(jnp.bfloat16)


def channelize(samples, gains):
    by_frame = jnp.transpose(samples.reshape(SHARE, SPEC + TAPS - 1, FRAME), (1, 0, 2))
    return pl.pallas_call(
        channelize_kernel,
        out_shape=jax.ShapeDtypeStruct((GROUPS, PER, SHARE, LANES), jnp.bfloat16),
        in_specs=[
            pl.BlockSpec(memory_space=pltpu.HBM),
            pl.BlockSpec(memory_space=pltpu.HBM),
            whole_vmem(),
        ],
        out_specs=whole_vmem(),
        scratch_shapes=[
            VMEM((SPEC + TAPS - 1, SHARE, FRAME), jnp.bfloat16),
            VMEM((GROUPS, 2 * PER, FRAME), jnp.bfloat16),
            VMEM((2, STEP // COL, SPEC * SHARE, COL), jnp.float32),
            VMEM((ROWS, SHARE * SPEC), jnp.float32),
            VMEM((ROWS * SHARE, SPEC), jnp.float32),
            VMEM((4 * TAPS, FRAME), jnp.bfloat16),
            VMEM((TAPS, FRAME), jnp.float32),
            pltpu.SemaphoreType.DMA((STEPS,)),
            pltpu.SemaphoreType.DMA,
            pltpu.SemaphoreType.DMA,
        ],
        compiler_params=pltpu.CompilerParams(vmem_limit_bytes=52 * MIB),
        name="channelize",
    )(by_frame, constant_tables(), gains)


def small_kernel(kernel, name, out_shape, *operands):
    return pl.pallas_call(
        kernel,
        out_shape=out_shape,
        in_specs=[whole_vmem()] * len(operands),
        out_specs=jax.tree.map(lambda _: whole_vmem(), out_shape),
        compiler_params=pltpu.CompilerParams(vmem_limit_bytes=16 * MIB),
        name=name,
    )(*operands)


def blocks(*lead):
    return jax.ShapeDtypeStruct((*lead, WIDTH, LANES), jnp.bfloat16)


def own_kernel(pieces, *outs):
    chunks, outgoing = outs[:CHUNKS], outs[CHUNKS:]
    for g in range(GROUPS):
        rows = slice(g * SHARE, (g + 1) * SHARE)
        for i in range(CHUNKS):
            for k in range(2):
                chunks[i][k, rows, :] = pieces[g, CHUNKS * k + i]
    theirs = 1 - far_half(blk_place()[0])
    for i in range(CHUNKS):
        outgoing[i // 2][i % 2] = chunks[i][theirs]


def own_chunks(pieces):
    shapes = (blocks(2),) * (CHUNKS + 2)
    return small_kernel(own_kernel, "own_chunks", shapes, pieces)


def pass_next(nexts, chosen):
    def kernel(*refs):
        theirs = 1 - far_half((blk_place()[0] + 3) % 4)
        for j in range(len(chosen)):
            refs[-1][j] = refs[j][theirs]

    return small_kernel(kernel, "pass_next", blocks(len(chosen)), *[nexts[i] for i in chosen])


def across_kernel(second, own, out):
    out[...] = jnp.where(blk_place()[1] == 0, second[...], own[...])


def for_across(second, own):
    return small_kernel(across_kernel, "for_across", blocks(2), second, own)


def pass_half_kernel(*refs):
    arrived, seconds, out = refs[:2], refs[2:-1], refs[-1]
    x, l = blk_place()
    for i in range(CHUNKS):
        out[i] = jnp.where(l == 0, arrived[i // 2][i % 2], seconds[i][far_half(x)])


def pass_half(arrived, seconds):
    return small_kernel(pass_half_kernel, "pass_half", blocks(CHUNKS), *arrived, *seconds)


def correlate_one(mine, other):
    crossed = jnp.concatenate([mine[:, SPEC:], -mine[:, :SPEC]], axis=1)
    contract = (((1,), (1,)), ((), ()))
    real = lax.dot_general(mine, other, contract, preferred_element_type=jnp.float32)
    imag = lax.dot_general(crossed, other, contract, preferred_element_type=jnp.float32)
    return (real * (1.0 / SPEC)).astype(jnp.bfloat16), (imag * (1.0 / SPEC)).astype(jnp.bfloat16)


def correlate(name, own, arrays, jobs, before, half_count, with_far=False):
    width, lanes = own[0].shape[1:]
    count = len(list(jobs(arrays, True)))

    def kernel(*refs):
        refs = list(refs)
        mine = [refs.pop(0) for _ in own]
        sources = [refs.pop(0) for _ in arrays]
        if before is not None:
            refs.pop(0)
        out = refs.pop(0)
        out_far = refs.pop(0) if with_far else None
        results, sems = refs
        copies = []
        for j, (i, k, other, offset) in enumerate(jobs(sources, False)):
            real, imag = correlate_one(mine[i][k], other)
            results[j, 0] = real
            results[j, 1] = imag
            target = out_far.at[i] if offset is None else out.at[offset, CHUNKS * k + i]
            copy = pltpu.make_async_copy(results.at[j], target, sems.at[j])
            copy.start()
            copies.append(copy)
        for copy in copies:
            copy.wait()

    near_shape = jax.ShapeDtypeStruct((half_count, PER, 2, width, width), jnp.bfloat16)
    far_shape = jax.ShapeDtypeStruct((CHUNKS, 2, width, width), jnp.bfloat16)
    operands = [*own, *arrays]
    specs = [whole_vmem()] * len(operands)
    aliases = {}
    if before is not None:
        aliases = {len(operands): 0}
        operands.append(before)
        specs.append(pl.BlockSpec(memory_space=pl.ANY))
    return pl.pallas_call(
        kernel,
        out_shape=(near_shape, far_shape) if with_far else near_shape,
        in_specs=specs,
        out_specs=(pl.BlockSpec(memory_space=pl.ANY),) * 2 if with_far else pl.BlockSpec(memory_space=pl.ANY),
        input_output_aliases=aliases,
        scratch_shapes=[VMEM((count, 2, width, width), jnp.bfloat16), pltpu.SemaphoreType.DMA((count,))],
        cost_estimate=pl.CostEstimate(
            flops=count * 4 * width * width * lanes,
            bytes_accessed=count * 4 * width * width,
            transcendentals=0,
        ),
        compiler_params=pltpu.CompilerParams(vmem_limit_bytes=24 * MIB),
        name=name,
    )(*operands)


def blk_route(step):
    return [(2 * x + l, step(x, l)) for x in range(4) for l in range(2)]


LEFT = blk_route(lambda x, l: 2 * ((x - 1) % 4) + l)
RIGHT = blk_route(lambda x, l: 2 * ((x + 1) % 4) + l)
SWAP = blk_route(lambda x, l: 2 * x + 1 - l)
LEFT_ODD = blk_route(lambda x, l: 2 * ((x - l) % 4) + l)


def send(block, axis, route):
    return lax.ppermute(block, axis, route)


def all_arrived(*arrays):
    return lax.optimization_barrier(arrays)


def on_device(samples, input_gains):
    half_count = lax.axis_size("blk") // 2
    last = CHUNKS - 1
    pieces = channelize(samples[0], input_gains[0])
    pieces = lax.all_to_all(pieces, "grp", split_axis=0, concat_axis=0, tiled=True)
    *own, out_a, out_b = own_chunks(pieces)
    leaving = list(own)
    across = send(own[last], "blk", SWAP)
    pass_a = send(out_a, "blk", RIGHT)
    pass_b = send(out_b, "blk", RIGHT)
    second, nexts = [], []
    for i in range(CHUNKS):
        second.append(send(leaving[i], "blk", LEFT))
        if i == 0:
            second[i], leaving[2], leaving[3] = all_arrived(second[i], leaving[2], leaving[3])
        if i == 1:
            second[i], pass_a = all_arrived(second[i], pass_a)
        if i == 2:
            second[i], *nexts = all_arrived(second[i], *nexts)
        if i == 1:
            _, _, pass_b = all_arrived(second[0], second[1], pass_b)
        if i < last:
            nexts.append(send(for_across(second[i], own[i]), "blk", SWAP))
    nexts.append(send(across, "blk", LEFT_ODD))
    arrived = [send(pass_a, "blk", RIGHT), send(pass_b, "blk", RIGHT)]
    third_a = send(pass_next(nexts, (0, 1)), "blk", LEFT)
    third_b = send(pass_next(nexts, (2, 3)), "blk", LEFT)
    third_half = send(pass_half(arrived, second), "blk", SWAP)

    def same(refs, counting):
        for i in range(CHUNKS):
            for k in range(2):
                yield i, k, None if counting else refs[i][k], 0

    def second_and_far(refs, counting):
        for i in range(CHUNKS):
            for k in range(2):
                yield i, k, None if counting else refs[i][k], 2
        half = None if counting else far_half(blk_place()[0])
        for i in range(CHUNKS):
            yield i, half, None if counting else refs[CHUNKS + i // 2][i % 2], None

    def first(refs, counting):
        for i in range(CHUNKS):
            for k in range(2):
                yield i, k, None if counting else refs[i][k], 1

    def third(refs, counting):
        half = None if counting else far_half(blk_place()[0])
        for i in range(CHUNKS):
            yield i, None if counting else 1 - half, None if counting else refs[i // 2][i % 2], 3
        for i in range(CHUNKS):
            yield i, half, None if counting else refs[2][i], 3

    vis_near = correlate("correlate_same", own, own, same, None, half_count)
    vis_near, vis_far = correlate(
        "correlate_second", own, [*second, *arrived], second_and_far, vis_near, half_count, True
    )
    vis_near = correlate("correlate_first", own, nexts, first, vis_near, half_count)
    vis_near = correlate("correlate_third", own, [third_a, third_b, third_half], third, vis_near, half_count)
    return (vis_near, vis_far)


def solution(mesh):
    return jax.shard_map(
        on_device,
        mesh=mesh,
        in_specs=(P("blk", "grp", None), P("blk", "grp", None)),
        out_specs=(P(None, "grp", None, "blk", None), P("grp", None, "blk", None)),
        check_vma=False,
    )
```
